256 devices in a mesh: row: 8 (over z_hi, core), col: 32 (over x, z_lo, y).
Axes of the slice: x: 4, y: 4, z: 8 (z_hi: 4, z_lo: 2; z = z_hi * 2 + z_lo), core: 2. Of those that a mesh axis runs over, the one named last changes fastest.
Arguments:
- object_field: float32 [2, 2, 4096, 8192], P(None, None, 'row', 'col'), may hold values from -4 to 4
- probe: float32 [2, 256, 256], replicated, may hold values from -4 to 4
- prop_phase: float32 [256, 256], replicated, may hold values from -3.140625 to 3.140625
- slot_count: int32 [8, 32], P('row', 'col'), may hold values from 1 to 4, as said below
- slot_offset: int32 [8, 32, 4, 2], P('row', 'col'), may hold values from 0 to 511, as said below
- intensity: float32 [8, 32, 4, 256, 256], P('row', 'col'), may hold values from 0.2 to 3
Outputs:
- object_grad: float32 [2, 2, 4096, 8192], P(None, None, 'row', 'col')
- probe_grad: float32 [2, 256, 256], replicated
The draws below stay inside these ranges and needn't reach their ends.
Inputs may be any that keep to these rules, and one draw needn't show every extreme that they name: `slot_count`: each tile owns 1 to 4 live scan positions; in every draw some tile owns 4, and most own one or two. `slot_offset`: row offsets are below 512 and column offsets below 256; every slot's 256 x 256 window lies inside the object, so it reaches at most into the tiles below, to the right and diagonally below right.
All inputs are finite; a program needn't handle non-finite values.
Results may differ from the reference program's by a relative error of at most 0.00015.
Values sent between devices are 32-bit elements; how exact they have to be, the bound alone decides.
No kernel may reach another device: no remote copies, remote signals or barrier semaphores. Data moves between devices by JAX's collectives and lax.ppermute only.
A program may use at most 128 MiB of HBM per device.

```python
import math
import jax
import jax.numpy as jnp
from jax import lax

W = 256
SLICES = 2
CAP = 4
TR = 512
TC = 256
GRID_R = 8
GRID_C = 32
NR = 4096
NC = 8192


def draw_slot_count(key, part):
    key = jax.random.fold_in(key, 11)
    heavy_key, light_key, row_key, col_key = jax.random.split(key, 4)
    heavy = jax.random.randint(heavy_key, (GRID_R, GRID_C), 0, 4) == 0
    light = jax.random.randint(light_key, (GRID_R, GRID_C), 1, 3)
    counts = jnp.where(heavy, CAP, light).astype(jnp.int32)
    pick_row = jax.random.randint(row_key, (), 0, GRID_R)
    pick_col = jax.random.randint(col_key, (), 0, GRID_C)
    return counts.at[pick_row, pick_col].set(CAP)


def draw_slot_offset(key, part):
    key = jax.random.fold_in(key, 23)
    row_key, col_key = jax.random.split(key, 2)
    row_limit = jnp.where(jnp.arange(GRID_R) == GRID_R - 1, TR - W + 1, TR)[:, None, None]
    col_limit = jnp.where(jnp.arange(GRID_C) == GRID_C - 1, TC - W + 1, TC)[None, :, None]
    shape = (GRID_R, GRID_C, CAP)
    row_offsets = jax.random.randint(row_key, shape, 0, jnp.broadcast_to(row_limit, shape))
    col_offsets = jax.random.randint(col_key, shape, 0, jnp.broadcast_to(col_limit, shape))
    row_offsets = row_offsets.at[0, 0, 0].set(TR - 1)
    col_offsets = col_offsets.at[0, 0, 0].set(TC - 1)
    return jnp.stack([row_offsets, col_offsets], axis=-1).astype(jnp.int32)


def block_levels(rng, dims, shards, low, high):
    loudness = 1.0
    for axis_at, shards_of in shards:
        heights = jax.random.uniform(jax.random.fold_in(jax.random.fold_in(rng, 6), axis_at), (shards_of,), jnp.float32, low / len(shards), high / len(shards))
        loudness = loudness * jnp.repeat(jnp.exp(heights), dims[axis_at] // shards_of).reshape((-1,) + (1,) * (len(dims) - 1 - axis_at))
    return loudness


def centred(stream_key, shape, scale, bound, cuts=(), held_as=jnp.bfloat16):
    drawn = scale * jax.random.normal(stream_key, shape, jnp.float32)
    if cuts:
        drawn = drawn * block_levels(stream_key, shape, cuts, -0.22, 0.18)
    return jnp.clip(drawn, -bound, bound).astype(held_as)


def setup_inputs(seed: int = 0) -> dict:
    key_list = jax.random.split(jax.random.key(seed), 7)
    return {
        "object_field": centred(key_list[0], (SLICES, 2, NR, NC), 0.7, 4.0, ((2, 8), (3, 32)), jnp.float32),
        "probe": centred(key_list[1], (2, W, W), 0.7, 4.0, (), jnp.float32),
        "prop_phase": jnp.clip(jax.random.uniform(key_list[2], (W, W), jnp.float32, -3.140625, 3.140625), -3.140625, 3.140625),
        "slot_count": draw_slot_count(jax.random.fold_in(key_list[6], 71), 0),
        "slot_offset": draw_slot_offset(jax.random.fold_in(key_list[6], 71), 0),
        "intensity": jnp.clip(jnp.exp(math.log(3.0) - 2.7080502 * jax.random.uniform(key_list[5], (GRID_R, GRID_C, CAP, W, W), jnp.float32) ** block_levels(key_list[5], (GRID_R, GRID_C, CAP, W, W), ((0, 8), (1, 32)), -0.2, 0.2)), 0.2, 3.0),
    }


def forward_backward(layers, probe_wave, kernel, measured):
    slices = layers.shape[0]
    incoming = [probe_wave]
    wave = probe_wave * layers[0]
    for index in range(1, slices):
        arriving = jnp.fft.ifft2(kernel * jnp.fft.fft2(wave, norm="ortho"), norm="ortho")
        incoming.append(arriving)
        wave = arriving * layers[index]
    far_field = jnp.fft.fft2(wave, norm="ortho")
    misfit = jnp.real(far_field) ** 2 + jnp.imag(far_field) ** 2 - measured
    adjoint = jnp.fft.ifft2(misfit * far_field, norm="ortho")
    gradients = [None] * slices
    for index in reversed(range(slices)):
        gradients[index] = jnp.conj(incoming[index]) * adjoint
        adjoint = jnp.conj(layers[index]) * adjoint
        if index > 0:
            adjoint = jnp.fft.ifft2(jnp.conj(kernel) * jnp.fft.fft2(adjoint, norm="ortho"), norm="ortho")
    return jnp.stack(gradients), adjoint


def reference(object_field, probe, prop_phase, slot_count, slot_offset, intensity):
    complex_object = object_field[:, 0] + 1j * object_field[:, 1]
    padded = jnp.pad(complex_object, ((0, 0), (0, W), (0, W)))
    probe_wave = probe[0] + 1j * probe[1]
    kernel = jnp.cos(prop_phase) + 1j * jnp.sin(prop_phase)
    row_starts = (jnp.arange(GRID_R, dtype=jnp.int32) * TR)[:, None, None] + slot_offset[..., 0]
    col_starts = (jnp.arange(GRID_C, dtype=jnp.int32) * TC)[None, :, None] + slot_offset[..., 1]
    live = jnp.arange(CAP, dtype=jnp.int32)[None, None, :] < slot_count[..., None]
    factors = jnp.where(live, 1.0, 0.0).astype(object_field.dtype)
    positions = GRID_R * GRID_C * CAP
    items = (row_starts.reshape(positions).astype(jnp.int32), col_starts.reshape(positions).astype(jnp.int32),
             factors.reshape(positions), intensity.reshape(positions, W, W))

    def visit(carry, item):
        object_total, probe_total = carry
        row_start, col_start, factor, measured = item
        start = (jnp.int32(0), row_start, col_start)
        layers = lax.dynamic_slice(padded, start, (SLICES, W, W))
        gradients, probe_term = forward_backward(layers, probe_wave, kernel, measured)
        current = lax.dynamic_slice(object_total, start, (SLICES, W, W))
        object_total = lax.dynamic_update_slice(object_total, current + factor * gradients, start)
        return (object_total, probe_total + factor * probe_term), None

    initial = (jnp.zeros_like(padded), jnp.zeros_like(probe_wave))
    (object_total, probe_total), unused = lax.scan(visit, initial, items)
    cropped = object_total[:, :NR, :NC]
    object_grad = jnp.stack([jnp.real(cropped), jnp.imag(cropped)], axis=1)
    probe_grad = jnp.stack([jnp.real(probe_total), jnp.imag(probe_total)])
    return object_grad, probe_grad
```

```python
import math

import jax
import jax.numpy as jnp
import ml_dtypes
import numpy as np
from jax import lax
from jax.experimental import pallas as pl
from jax.experimental.pallas import tpu as pltpu
from jax.sharding import PartitionSpec as P

VMEM = pltpu.VMEM
SMEM = pltpu.SMEM
LIMIT = 40 * 1024 * 1024


def dft_blocks(window):
    indices = np.arange(window)
    angles = 2.0 * math.pi / window * (indices[:, None] * indices[None, :] % window)
    cos, sin = np.cos(angles) / math.sqrt(window), np.sin(angles) / math.sqrt(window)
    ahead = np.block([[cos, -sin], [sin, cos]])
    behind = np.block([[cos, sin], [-sin, cos]])
    parts = []
    for table in (ahead, behind):
        high = table.astype(ml_dtypes.bfloat16)
        low = (table - high.astype(np.float64)).astype(ml_dtypes.bfloat16)
        parts.append(np.stack([high, low]))
    return np.stack(parts)


def halves(value):
    high = value.astype(jnp.bfloat16)
    return high, (value - high.astype(jnp.float32)).astype(jnp.bfloat16)


def dot(left, right):
    return jnp.dot(left, right, preferred_element_type=jnp.float32)


def along_columns(wave, table):
    window = wave[0].shape[0]
    high, low = halves(jnp.concatenate(wave, axis=1))
    out = dot(high, table[0]) + dot(low, table[0]) + dot(high, table[1])
    return out[:, :window], out[:, window:]


def along_rows(wave, table):
    window = wave[0].shape[0]
    high, low = halves(jnp.concatenate(wave, axis=0))
    out = dot(table[0], high) + dot(table[0], low) + dot(table[1], high)
    return out[:window], out[window:]


def forward(wave, tables):
    return along_rows(along_columns(wave, tables.at[0]), tables.at[1])


def inverse(wave, tables):
    return along_rows(along_columns(wave, tables.at[1]), tables.at[0])


def product(first, second):
    return (
        first[0] * second[0] - first[1] * second[1],
        first[0] * second[1] + first[1] * second[0],
    )


def conjugate_product(first, second):
    return (
        first[0] * second[0] + first[1] * second[1],
        first[0] * second[1] - first[1] * second[0],
    )


def corner(offsets, slot, window):
    row, column = offsets[slot, 0], offsets[slot, 1]
    block = row // window
    rows = lax.broadcasted_iota(jnp.int32, (window, window), 0)
    columns = lax.broadcasted_iota(jnp.int32, (window, window), 1)
    row = row - block * window
    return block, row, column, rows >= row, columns >= column


def cut(place, own, right_top, right_bottom, below, diagonal, window):
    block, _, _, upper, left = place
    first = block == 0
    out = []
    for part in range(2):
        own_top, own_bottom = own[part, :window], own[part, window:]
        top = jnp.where(
            left,
            jnp.where(first, own_top, own_bottom),
            jnp.where(first, right_top[part], right_bottom[part]),
        )
        bottom = jnp.where(
            left,
            jnp.where(first, own_bottom, below[part]),
            jnp.where(first, right_bottom[part], diagonal[part]),
        )
        out.append(jnp.where(upper, top, bottom))
    return tuple(out)


def deposit(place, total, term):
    block, _, _, upper, left = place
    for part in range(2):
        value = term[part]
        top = jnp.where(upper, value, 0.0)
        bottom = value - top
        for rows, piece in ((block, top), (block + 1, bottom)):
            kept = jnp.where(left, piece, 0.0)
            total[0, rows, part] += kept
            total[1, rows, part] += piece - kept


def shifted(wave, row, column):
    return tuple(pltpu.roll(pltpu.roll(part, row, 0), column, 1) for part in wave)


def arrive_kernel(
    count, offsets, own, right_top, right_bottom, below, diagonal, probe, kernel, tables, arriving
):
    window = probe.shape[-1]
    slot = pl.program_id(0)

    @pl.when(slot < count[0, 0])
    def _():
        place = corner(offsets, slot, window)
        layer = cut(place, own.at[0], right_top, right_bottom, below, diagonal, window)
        incoming = shifted((probe[0], probe[1]), place[1], place[2])
        spectrum = forward(product(incoming, layer), tables)
        out = inverse(product((kernel[0], kernel[1]), spectrum), tables)
        arriving[0, 0], arriving[0, 1] = out


def misfit_kernel(
    count, offsets, own, right_top, right_bottom, below, diagonal, arriving, measured, tables,
    total, leaving,
):
    window = measured.shape[-1]
    slot = pl.program_id(0)

    @pl.when(slot == 0)
    def _():
        total[...] = jnp.zeros_like(total)

    @pl.when(slot < count[0, 0])
    def _():
        place = corner(offsets, slot, window)
        layer = cut(place, own.at[0], right_top, right_bottom, below, diagonal, window)
        wave = (arriving[0, 0], arriving[0, 1])
        far = forward(product(wave, layer), tables)
        misfit = far[0] * far[0] + far[1] * far[1] - measured[0]
        adjoint = inverse((misfit * far[0], misfit * far[1]), tables)
        deposit(place, total, conjugate_product(wave, adjoint))
        out = conjugate_product(layer, adjoint)
        leaving[0, 0], leaving[0, 1] = out


def leave_kernel(
    count, offsets, own, right_top, right_bottom, below, diagonal, probe, kernel, leaving, tables,
    total, probe_total,
):
    window = probe.shape[-1]
    slot = pl.program_id(0)

    @pl.when(slot == 0)
    def _():
        total[...] = jnp.zeros_like(total)
        probe_total[...] = jnp.zeros_like(probe_total)

    @pl.when(slot < count[0, 0])
    def _():
        place = corner(offsets, slot, window)
        layer = cut(place, own.at[0], right_top, right_bottom, below, diagonal, window)
        incoming = shifted((probe[0], probe[1]), place[1], place[2])
        spectrum = forward((leaving[0, 0], leaving[0, 1]), tables)
        adjoint = inverse(conjugate_product((kernel[0], kernel[1]), spectrum), tables)
        deposit(place, total, conjugate_product(incoming, adjoint))
        term = conjugate_product(layer, adjoint)
        term = shifted(term, (window - place[1]) % window, (window - place[2]) % window)
        probe_total[0] += term[0]
        probe_total[1] += term[1]


def whole(shape):
    return pl.BlockSpec(shape, lambda slot: (0,) * len(shape))


def call(body, capacity, window, layer, operands, specs, outs, out_specs, name):
    block = (2, window, window)
    passes = 2 * 24 * 2 * window**3
    return pl.pallas_call(
        body,
        grid=(capacity,),
        in_specs=[
            pl.BlockSpec(memory_space=SMEM),
            pl.BlockSpec(memory_space=SMEM),
            pl.BlockSpec((1, 2, 2 * window, window), lambda slot: (layer, 0, 0, 0)),
            whole(block),
            whole(block),
            whole(block),
            whole(block),
            *specs,
        ],
        out_shape=outs,
        out_specs=out_specs,
        name=name,
        compiler_params=pltpu.CompilerParams(vmem_limit_bytes=LIMIT),
        cost_estimate=pl.CostEstimate(
            flops=capacity * passes, bytes_accessed=8 * 1024 * 1024, transcendentals=0
        ),
    )(*operands)


def from_behind(value, axis, steps):
    count = lax.axis_size(axis)
    leading, last = (max(0, -steps), min(count, count - steps))
    return lax.ppermute(value, axis, [(source, source + steps) for source in range(leading, last)])


def exchange(value, axis, bit):
    return lax.ppermute(value, axis, [(i, i ^ bit) for i in range(lax.axis_size(axis))])


def sum_everywhere(value):
    shape = value.shape
    value = value.reshape(-1, shape[-1])
    scattered = (("row", 1), ("col", 1), ("col", 8))
    whole_sums = (("col", 2), ("col", 16), ("col", 4), ("row", 2), ("row", 4))
    for axis, bit in scattered:
        first = lax.axis_index(axis) & bit == 0
        low, high = jnp.split(value, 2)
        kept, sent = jnp.where(first, low, high), jnp.where(first, high, low)
        value = kept + exchange(sent, axis, bit)
    for axis, bit in whole_sums:
        value = value + exchange(value, axis, bit)
    for axis, bit in reversed(scattered):
        first = lax.axis_index(axis) & bit == 0
        other = exchange(value, axis, bit)
        value = jnp.concatenate([jnp.where(first, value, other), jnp.where(first, other, value)])
    return value.reshape(shape)


def per_device(object_field, probe, prop_phase, slot_count, slot_offset, intensity):
    window = probe.shape[-1]
    capacity = intensity.shape[2]
    offsets = slot_offset[0, 0]
    measured = intensity[0, 0]
    tables = jnp.asarray(dft_blocks(window))
    kernel = jnp.stack([jnp.cos(prop_phase), jnp.sin(prop_phase)])
    block = (2, window, window)
    f32 = jnp.float32
    per_slot = jax.ShapeDtypeStruct((capacity, *block), f32)
    slot_spec = pl.BlockSpec((1, *block), lambda slot: (slot, 0, 0, 0))
    table_spec = whole(tables.shape)
    total_shape = (2, 3, *block)
    total = jax.ShapeDtypeStruct(total_shape, f32)

    def halo(layer):
        top, bottom = object_field[layer, :, :window], object_field[layer, :, window:]
        right_top = from_behind(top, "col", -1)
        below = from_behind(top, "row", -1)
        right_bottom = from_behind(bottom, "col", -1)
        diagonal = from_behind(right_top, "row", -1)
        return right_top, right_bottom, below, diagonal

    def gather(total):
        own, right = total[0], total[1]
        below = from_behind(own[2], "row", 1)
        diagonal = from_behind(right[2], "row", 1)
        from_left_top = from_behind(right[0] + diagonal, "col", 1)
        from_left_bottom = from_behind(right[1], "col", 1)
        return jnp.concatenate([own[0] + below + from_left_top, own[1] + from_left_bottom], axis=1)

    near = halo(0)
    far = halo(1)
    first = (slot_count, offsets, object_field)
    arriving = call(
        arrive_kernel, capacity, window, 0,
        (*first, *near, probe, kernel, tables),
        (whole(block), whole(block), table_spec),
        per_slot, slot_spec, "arrive",
    )
    last_total, leaving = call(
        misfit_kernel, capacity, window, 1,
        (*first, *far, arriving, measured, tables),
        (slot_spec, pl.BlockSpec((1, window, window), lambda slot: (slot, 0, 0)), table_spec),
        (total, per_slot), (whole(total_shape), slot_spec), "misfit",
    )
    first_total, probe_total = call(
        leave_kernel, capacity, window, 0,
        (*first, *near, probe, kernel, leaving, tables),
        (whole(block), whole(block), slot_spec, table_spec),
        (total, jax.ShapeDtypeStruct(block, f32)), (whole(total_shape), whole(block)), "leave",
    )
    last_grad = gather(last_total)
    first_grad = gather(first_total)
    probe_grad = sum_everywhere(probe_total)
    return (jnp.stack([first_grad, last_grad]), probe_grad)


def solution(mesh):
    return jax.shard_map(
        per_device,
        mesh=mesh,
        in_specs=(
            P(None, None, "row", "col"),
            P(),
            P(),
            P("row", "col"),
            P("row", "col", None, None),
            P("row", "col", None, None, None),
        ),
        out_specs=(P(None, None, "row", "col"), P()),
        check_vma=False,
    )
```

```python
import math

import jax
import jax.numpy as jnp
import ml_dtypes
import numpy as np
from jax import lax
from jax.experimental import pallas as pl
from jax.experimental.pallas import tpu as pltpu
from jax.sharding import PartitionSpec as P

VMEM = pltpu.VMEM
SMEM = pltpu.SMEM
LIMIT = 40 * 1024 * 1024


def dft_blocks(window):
    half = window // 2
    places, turns = np.arange(half)[:, None], np.arange(half)[None, :]
    forms = []
    for parity in range(2):
        angles = 2.0 * math.pi / window * (places * (2 * turns + parity) % window)
        cos, sin = np.cos(angles) / math.sqrt(window), np.sin(angles) / math.sqrt(window)
        forms.append(np.block([[cos, -sin], [sin, cos]]))
    tables = []
    for form in (forms, [np.transpose(form) for form in forms]):
        form = np.stack(form)
        high = form.astype(ml_dtypes.bfloat16)
        low = (form - high.astype(np.float64)).astype(ml_dtypes.bfloat16)
        tables.append(np.stack([high, low], axis=1))
    return np.stack(tables)


def halves(value):
    high = value.astype(jnp.bfloat16)
    return high, (value - high.astype(jnp.float32)).astype(jnp.bfloat16)


def dot(left, right):
    return jnp.dot(left, right, preferred_element_type=jnp.float32)


def apply(value, table, axis):
    high, low = halves(value)
    if axis:
        return dot(high, table[0]) + dot(low, table[0]) + dot(high, table[1])
    return dot(table[0], high) + dot(table[0], low) + dot(table[1], high)


def cleave(value, axis):
    half = value.shape[axis] // 2
    if axis:
        return value[:, :half], value[:, half:]
    return value[:half], value[half:]


def apart(wave, tables, axis):
    pairs = [cleave(part, axis) for part in wave]
    even = jnp.concatenate([first + second for first, second in pairs], axis=axis)
    odd = jnp.concatenate([first - second for first, second in pairs], axis=axis)
    even = cleave(apply(even, tables.at[0], axis), axis)
    odd = cleave(apply(odd, tables.at[1], axis), axis)
    return tuple(jnp.concatenate(pair, axis=axis) for pair in zip(even, odd))


def together(wave, tables, axis):
    even, odd = zip(*(cleave(part, axis) for part in wave))
    even = cleave(apply(jnp.concatenate(even, axis=axis), tables.at[0], axis), axis)
    odd = cleave(apply(jnp.concatenate(odd, axis=axis), tables.at[1], axis), axis)
    return tuple(
        jnp.concatenate([first + second, first - second], axis=axis)
        for first, second in zip(even, odd)
    )


def forward(wave, tables):
    return apart(apart(wave, tables.at[0], 1), tables.at[1], 0)


def inverse(wave, tables):
    return together(together(wave, tables.at[1], 1), tables.at[0], 0)


def reorder_kernel(image, pick, out):
    def moved(value, axis):
        total = None
        for _ in range(3):
            term = value.astype(jnp.bfloat16)
            value = value - term.astype(jnp.float32)
            term = dot(term, pick[1]) if axis else dot(pick[0], term)
            total = term if total is None else total + term
        return total

    out[0] = moved(moved(image[0], 1), 0)


def reorder(images):
    count, window, _ = images.shape
    order = np.concatenate([np.arange(0, window, 2), np.arange(1, window, 2)])
    pick = np.eye(window)[order]
    pick = jnp.asarray(np.stack([pick, pick.T]).astype(ml_dtypes.bfloat16))
    spec = pl.BlockSpec((1, window, window), lambda image: (image, 0, 0))
    return pl.pallas_call(
        reorder_kernel,
        grid=(count,),
        in_specs=[spec, whole(pick.shape)],
        out_specs=spec,
        out_shape=jax.ShapeDtypeStruct(images.shape, jnp.float32),
        name="reorder",
        compiler_params=pltpu.CompilerParams(vmem_limit_bytes=LIMIT),
        cost_estimate=pl.CostEstimate(
            flops=count * 12 * window**3, bytes_accessed=8 * images.size, transcendentals=0
        ),
    )(images, pick)


def product(first, second):
    return (
        first[0] * second[0] - first[1] * second[1],
        first[0] * second[1] + first[1] * second[0],
    )


def conjugate_product(first, second):
    return (
        first[0] * second[0] + first[1] * second[1],
        first[0] * second[1] - first[1] * second[0],
    )


def corner(offsets, slot, window):
    row, column = offsets[slot, 0], offsets[slot, 1]
    block = row // window
    rows = lax.broadcasted_iota(jnp.int32, (window, window), 0)
    columns = lax.broadcasted_iota(jnp.int32, (window, window), 1)
    row = row - block * window
    return block, row, column, rows >= row, columns >= column


def cut(place, own, right_top, right_bottom, below, diagonal, window):
    block, _, _, upper, left = place
    first = block == 0
    out = []
    for part in range(2):
        own_top, own_bottom = own[part, :window], own[part, window:]
        top = jnp.where(
            left,
            jnp.where(first, own_top, own_bottom),
            jnp.where(first, right_top[part], right_bottom[part]),
        )
        bottom = jnp.where(
            left,
            jnp.where(first, own_bottom, below[part]),
            jnp.where(first, right_bottom[part], diagonal[part]),
        )
        out.append(jnp.where(upper, top, bottom))
    return tuple(out)


def deposit(place, total, term):
    block, _, _, upper, left = place
    for part in range(2):
        value = term[part]
        top = jnp.where(upper, value, 0.0)
        bottom = value - top
        for rows, piece in ((block, top), (block + 1, bottom)):
            kept = jnp.where(left, piece, 0.0)
            total[rows, 0, part] += kept
            total[rows, 1, part] += piece - kept


def shifted(wave, row, column):
    return tuple(pltpu.roll(pltpu.roll(part, row, 0), column, 1) for part in wave)


def arrive_kernel(
    count, offsets, own, right_top, right_bottom, below, diagonal, probe, kernel, tables, arriving
):
    window = probe.shape[-1]
    slot = pl.program_id(0)

    @pl.when(slot < count[0, 0])
    def _():
        place = corner(offsets, slot, window)
        layer = cut(place, own.at[0], right_top, right_bottom, below, diagonal, window)
        incoming = shifted((probe[0], probe[1]), place[1], place[2])
        spectrum = forward(product(incoming, layer), tables)
        out = inverse(product((kernel[0], kernel[1]), spectrum), tables)
        arriving[0, 0], arriving[0, 1] = out


def misfit_kernel(
    count, offsets, own, right_top, right_bottom, below, diagonal, arriving, measured, tables,
    total, leaving,
):
    window = measured.shape[-1]
    slot = pl.program_id(0)

    @pl.when(slot == 0)
    def _():
        total[...] = jnp.zeros_like(total)

    @pl.when(slot < count[0, 0])
    def _():
        place = corner(offsets, slot, window)
        layer = cut(place, own.at[0], right_top, right_bottom, below, diagonal, window)
        wave = (arriving[0, 0], arriving[0, 1])
        far = forward(product(wave, layer), tables)
        misfit = far[0] * far[0] + far[1] * far[1] - measured[0]
        adjoint = inverse((misfit * far[0], misfit * far[1]), tables)
        deposit(place, total, conjugate_product(wave, adjoint))
        out = conjugate_product(layer, adjoint)
        leaving[0, 0], leaving[0, 1] = out


def leave_kernel(
    count, offsets, own, right_top, right_bottom, below, diagonal, probe, kernel, leaving, tables,
    total, probe_total,
):
    window = probe.shape[-1]
    slot = pl.program_id(0)

    @pl.when(slot == 0)
    def _():
        total[...] = jnp.zeros_like(total)
        probe_total[...] = jnp.zeros_like(probe_total)

    @pl.when(slot < count[0, 0])
    def _():
        place = corner(offsets, slot, window)
        layer = cut(place, own.at[0], right_top, right_bottom, below, diagonal, window)
        incoming = shifted((probe[0], probe[1]), place[1], place[2])
        spectrum = forward((leaving[0, 0], leaving[0, 1]), tables)
        adjoint = inverse(conjugate_product((kernel[0], kernel[1]), spectrum), tables)
        deposit(place, total, conjugate_product(incoming, adjoint))
        term = conjugate_product(layer, adjoint)
        term = shifted(term, (window - place[1]) % window, (window - place[2]) % window)
        probe_total[0] += term[0]
        probe_total[1] += term[1]


def whole(shape):
    return pl.BlockSpec(shape, lambda slot: (0,) * len(shape))


def call(body, capacity, window, layer, operands, specs, outs, out_specs, name, weight=1):
    block = (2, window, window)
    passes = weight * 2 * 12 * 2 * window**3
    return pl.pallas_call(
        body,
        grid=(capacity,),
        in_specs=[
            pl.BlockSpec(memory_space=SMEM),
            pl.BlockSpec(memory_space=SMEM),
            pl.BlockSpec((1, 2, 2 * window, window), lambda slot: (layer, 0, 0, 0)),
            whole(block),
            whole(block),
            whole(block),
            whole(block),
            *specs,
        ],
        out_shape=outs,
        out_specs=out_specs,
        name=name,
        compiler_params=pltpu.CompilerParams(vmem_limit_bytes=LIMIT),
        cost_estimate=pl.CostEstimate(
            flops=capacity * passes, bytes_accessed=8 * 1024 * 1024, transcendentals=0
        ),
    )(*operands)


def from_behind(value, axis, steps):
    count = lax.axis_size(axis)
    leading, last = (max(0, -steps), min(count, count - steps))
    return lax.ppermute(value, axis, [(source, source + steps) for source in range(leading, last)])


def around(value, steps):
    count = lax.axis_size("col")
    return lax.ppermute(value, "col", [(i, i // 4 * 4 + (i + steps) % 4) for i in range(count)])


def across(value, moved, steps):
    edge = 3 if steps < 0 else 0
    count = lax.axis_size("col")
    pairs = [(i, i + 4 * steps) for i in range(edge, count, 4) if 0 <= i + 4 * steps < count]
    passed = lax.ppermute(value, "col", pairs)
    return jnp.where(lax.axis_index("col") % 4 == edge, passed, moved)


def after(value, *earlier):
    for other in earlier:
        value = value + 0.0 * other[(0,) * other.ndim]
    return value


def exchange(value, axis, bit):
    return lax.ppermute(value, axis, [(i, i ^ bit) for i in range(lax.axis_size(axis))])


def bits(axis, low):
    place = lax.axis_index(axis)
    return place & low != 0, place & (2 * low) != 0


def ordered(pieces, swaps):
    for step, swap in zip((1, 2), swaps):
        pieces = [jnp.where(swap, pieces[k ^ step], pieces[k]) for k in range(len(pieces))]
    return pieces


def sum_everywhere(value, waits):
    shape = value.shape
    value = value.reshape(-1, shape[-1])
    core = lax.axis_index("row") & 1 != 0
    low, high = jnp.split(value, 2)
    value = jnp.where(core, high, low) + exchange(jnp.where(core, low, high), "row", 1)
    value = after(value, *waits[0])
    swaps = bits("col", 8)
    parts = ordered(jnp.split(value, 4), swaps)
    others = [exchange(parts[k], "col", 8 * k) for k in (1, 2, 3)]
    value = (parts[0] + others[0]) + (others[1] + others[2])
    for at, (axis, low) in enumerate((("col", 1), ("row", 2))):
        value = after(value, *waits[at + 1])
        others = [exchange(value, axis, k * low) for k in (1, 2, 3)]
        value = (value + others[0]) + (others[1] + others[2])
    value = value + exchange(value, "col", 4)
    value = after(value, *waits[3])
    others = [exchange(value, "col", 8 * k) for k in (1, 2, 3)]
    value = jnp.concatenate(ordered([value, *others], swaps))
    other = exchange(value, "row", 1)
    value = jnp.concatenate([jnp.where(core, other, value), jnp.where(core, value, other)])
    return value.reshape(shape)


def per_device(object_field, probe, prop_phase, slot_count, slot_offset, intensity):
    window = probe.shape[-1]
    capacity = intensity.shape[2]
    offsets = slot_offset[0, 0]
    measured = reorder(intensity[0, 0])
    prop_phase = reorder(prop_phase[None])[0]
    tables = jnp.asarray(dft_blocks(window))
    kernel = jnp.stack([jnp.cos(prop_phase), jnp.sin(prop_phase)])
    block = (2, window, window)
    f32 = jnp.float32
    per_slot = jax.ShapeDtypeStruct((capacity, *block), f32)
    slot_spec = pl.BlockSpec((1, *block), lambda slot: (slot, 0, 0, 0))
    table_spec = whole(tables.shape)
    total_shape = (3, 2, *block)
    total = jax.ShapeDtypeStruct(total_shape, f32)

    rows, columns = lax.axis_size("row"), lax.axis_size("col")

    def between(value, move):
        pairs = []
        for row in range(rows):
            for column in range(columns):
                to_row, to_column = move(row, column)
                if 0 <= to_row < rows and 0 <= to_column < columns:
                    pairs.append((row * columns + column, to_row * columns + to_column))
        return lax.ppermute(value, ("row", "col"), pairs)

    def halo(field):
        top, bottom = field[:, :, :window], field[:, :, window:]
        right_top = from_behind(top, "col", -1)
        below = from_behind(top, "row", -1)
        moved = around(bottom, -1)
        near_corner = between(right_top, lambda r, c: (r - 1 if r % 2 else -1, c))
        far_corner = between(below, lambda r, c: (r if r % 2 else -1, c - 1))
        right_bottom = across(moved, moved, -1)
        return right_top, right_bottom, below, near_corner + far_corner

    def send_down(total):
        return from_behind(total[2], "row", 1), around(total[1, 1], 1)

    near = tuple(part[0] for part in halo(object_field[:1]))
    far = tuple(part[0] for part in halo(object_field[1:]))
    first = (slot_count, offsets, object_field)
    arriving = call(
        arrive_kernel, capacity, window, 0,
        (*first, *near, probe, kernel, tables),
        (whole(block), whole(block), table_spec),
        per_slot, slot_spec, "arrive",
    )
    last_total, leaving = call(
        misfit_kernel, capacity, window, 1,
        (*first, *far, arriving, measured, tables),
        (slot_spec, pl.BlockSpec((1, window, window), lambda slot: (slot, 0, 0)), table_spec),
        (total, per_slot), (whole(total_shape), slot_spec), "misfit",
    )
    first_total, probe_total = call(
        leave_kernel, capacity, window, 0,
        (*first, *near, probe, kernel, leaving, tables),
        (whole(block), whole(block), slot_spec, table_spec),
        (total, jax.ShapeDtypeStruct(block, f32)), (whole(total_shape), whole(block)), "leave", 8,
    )
    def gather(total):
        down, moved = send_down(total)
        left_top = from_behind(total[0, 1] + down[1], "col", 1)
        left_bottom = across(moved, moved, 1)
        grad = [total[0, 0] + down[0] + left_top, total[1, 0] + left_bottom]
        return jnp.concatenate(grad, axis=1), (down, moved), (left_top, left_bottom)

    last_grad, last_down, last_over = gather(last_total)
    first_grad, first_down, first_over = gather(first_total)
    waits = ((last_down[0],), (first_down[1],), (first_down[0],), last_over)
    probe_grad = sum_everywhere(after(probe_total, last_down[1]), waits)
    return (jnp.stack([first_grad, last_grad]), probe_grad)


def solution(mesh):
    return jax.shard_map(
        per_device,
        mesh=mesh,
        in_specs=(
            P(None, None, "row", "col"),
            P(),
            P(),
            P("row", "col"),
            P("row", "col", None, None),
            P("row", "col", None, None, None),
        ),
        out_specs=(P(None, None, "row", "col"), P()),
        check_vma=False,
    )
```

```python
import math

import jax
import jax.numpy as jnp
import ml_dtypes
import numpy as np
from jax import lax
from jax.experimental import pallas as pl
from jax.experimental.pallas import tpu as pltpu
from jax.sharding import PartitionSpec as P

VMEM = pltpu.VMEM
SMEM = pltpu.SMEM
LIMIT = 40 * 1024 * 1024


def dft_blocks(window):
    half = window // 2
    places, turns = np.arange(half)[:, None], np.arange(half)[None, :]
    forms = []
    for parity in range(2):
        angles = 2.0 * math.pi / window * (places * (2 * turns + parity) % window)
        cos, sin = np.cos(angles) / math.sqrt(window), np.sin(angles) / math.sqrt(window)
        forms.append(np.block([[cos, -sin], [sin, cos]]))
    tables = []
    for form in (forms, [np.transpose(form) for form in forms]):
        form = np.stack(form)
        high = form.astype(ml_dtypes.bfloat16)
        low = (form - high.astype(np.float64)).astype(ml_dtypes.bfloat16)
        tables.append(np.stack([high, low], axis=1))
    return np.stack(tables)


def halves(value):
    high = value.astype(jnp.bfloat16)
    return high, (value - high.astype(jnp.float32)).astype(jnp.bfloat16)


def dot(left, right):
    return jnp.dot(left, right, preferred_element_type=jnp.float32)


def apply(value, table, axis):
    high, low = halves(value)
    if axis:
        return dot(high, table[0]) + dot(low, table[0]) + dot(high, table[1])
    return dot(table[0], high) + dot(table[0], low) + dot(table[1], high)


def cleave(value, axis):
    half = value.shape[axis] // 2
    if axis:
        return value[:, :half], value[:, half:]
    return value[:half], value[half:]


def apart(wave, tables, axis):
    pairs = [cleave(part, axis) for part in wave]
    even = jnp.concatenate([first + second for first, second in pairs], axis=axis)
    odd = jnp.concatenate([first - second for first, second in pairs], axis=axis)
    even = cleave(apply(even, tables.at[0], axis), axis)
    odd = cleave(apply(odd, tables.at[1], axis), axis)
    return tuple(jnp.concatenate(pair, axis=axis) for pair in zip(even, odd))


def together(wave, tables, axis):
    even, odd = zip(*(cleave(part, axis) for part in wave))
    even = cleave(apply(jnp.concatenate(even, axis=axis), tables.at[0], axis), axis)
    odd = cleave(apply(jnp.concatenate(odd, axis=axis), tables.at[1], axis), axis)
    return tuple(
        jnp.concatenate([first + second, first - second], axis=axis)
        for first, second in zip(even, odd)
    )


def forward(wave, tables):
    return apart(apart(wave, tables.at[0], 1), tables.at[1], 0)


def inverse(wave, tables):
    return together(together(wave, tables.at[1], 1), tables.at[0], 0)


def reorder_kernel(image, pick, out):
    def moved(value, axis):
        total = None
        for _ in range(3):
            term = value.astype(jnp.bfloat16)
            value = value - term.astype(jnp.float32)
            term = dot(term, pick[1]) if axis else dot(pick[0], term)
            total = term if total is None else total + term
        return total

    out[0] = moved(moved(image[0], 1), 0)


def reorder(images):
    count, window, _ = images.shape
    order = np.concatenate([np.arange(0, window, 2), np.arange(1, window, 2)])
    pick = np.eye(window)[order]
    pick = jnp.asarray(np.stack([pick, pick.T]).astype(ml_dtypes.bfloat16))
    spec = pl.BlockSpec((1, window, window), lambda image: (image, 0, 0))
    return pl.pallas_call(
        reorder_kernel,
        grid=(count,),
        in_specs=[spec, whole(pick.shape)],
        out_specs=spec,
        out_shape=jax.ShapeDtypeStruct(images.shape, jnp.float32),
        name="reorder",
        compiler_params=pltpu.CompilerParams(vmem_limit_bytes=LIMIT),
        cost_estimate=pl.CostEstimate(
            flops=count * 12 * window**3, bytes_accessed=8 * images.size, transcendentals=0
        ),
    )(images, pick)


def product(first, second):
    return (
        first[0] * second[0] - first[1] * second[1],
        first[0] * second[1] + first[1] * second[0],
    )


def conjugate_product(first, second):
    return (
        first[0] * second[0] + first[1] * second[1],
        first[0] * second[1] - first[1] * second[0],
    )


def corner(offsets, slot, window):
    row, column = offsets[slot, 0], offsets[slot, 1]
    block = row // window
    rows = lax.broadcasted_iota(jnp.int32, (window, window), 0)
    columns = lax.broadcasted_iota(jnp.int32, (window, window), 1)
    row = row - block * window
    return block, row, column, rows >= row, columns >= column


def cut(place, own, right_top, right_bottom, below, diagonal, window):
    block, _, _, upper, left = place
    first = block == 0
    out = []
    for part in range(2):
        own_top, own_bottom = own[part, :window], own[part, window:]
        top = jnp.where(
            left,
            jnp.where(first, own_top, own_bottom),
            jnp.where(first, right_top[part], right_bottom[part]),
        )
        bottom = jnp.where(
            left,
            jnp.where(first, own_bottom, below[part]),
            jnp.where(first, right_bottom[part], diagonal[part]),
        )
        out.append(jnp.where(upper, top, bottom))
    return tuple(out)


def deposit(place, total, term):
    block, _, _, upper, left = place
    for part in range(2):
        value = term[part]
        top = jnp.where(upper, value, 0.0)
        bottom = value - top
        for rows, piece in ((block, top), (block + 1, bottom)):
            kept = jnp.where(left, piece, 0.0)
            total[rows, 0, part] += kept
            total[rows, 1, part] += piece - kept


def shifted(wave, row, column):
    return tuple(pltpu.roll(pltpu.roll(part, row, 0), column, 1) for part in wave)


def arrive_kernel(
    count, offsets, own, right_top, right_bottom, below, diagonal, probe, kernel, tables, arriving
):
    window = probe.shape[-1]
    slot = pl.program_id(0)

    @pl.when(slot < count[0, 0])
    def _():
        place = corner(offsets, slot, window)
        layer = cut(place, own.at[0], right_top, right_bottom, below, diagonal, window)
        incoming = shifted((probe[0], probe[1]), place[1], place[2])
        spectrum = forward(product(incoming, layer), tables)
        out = inverse(product((kernel[0], kernel[1]), spectrum), tables)
        arriving[0, 0], arriving[0, 1] = out


def misfit_kernel(
    count, offsets, own, right_top, right_bottom, below, diagonal, arriving, measured, tables,
    total, leaving,
):
    window = measured.shape[-1]
    slot = pl.program_id(0)

    @pl.when(slot == 0)
    def _():
        total[...] = jnp.zeros_like(total)

    @pl.when(slot < count[0, 0])
    def _():
        place = corner(offsets, slot, window)
        layer = cut(place, own.at[0], right_top, right_bottom, below, diagonal, window)
        wave = (arriving[0, 0], arriving[0, 1])
        far = forward(product(wave, layer), tables)
        misfit = far[0] * far[0] + far[1] * far[1] - measured[0]
        adjoint = inverse((misfit * far[0], misfit * far[1]), tables)
        deposit(place, total, conjugate_product(wave, adjoint))
        out = conjugate_product(layer, adjoint)
        leaving[0, 0], leaving[0, 1] = out


def leave_kernel(
    count, offsets, own, right_top, right_bottom, below, diagonal, probe, kernel, leaving, tables,
    total, probe_total,
):
    window = probe.shape[-1]
    slot = pl.program_id(0)

    @pl.when(slot == 0)
    def _():
        total[...] = jnp.zeros_like(total)
        probe_total[...] = jnp.zeros_like(probe_total)

    @pl.when(slot < count[0, 0])
    def _():
        place = corner(offsets, slot, window)
        layer = cut(place, own.at[0], right_top, right_bottom, below, diagonal, window)
        incoming = shifted((probe[0], probe[1]), place[1], place[2])
        spectrum = forward((leaving[0, 0], leaving[0, 1]), tables)
        adjoint = inverse(conjugate_product((kernel[0], kernel[1]), spectrum), tables)
        deposit(place, total, conjugate_product(incoming, adjoint))
        term = conjugate_product(layer, adjoint)
        term = shifted(term, (window - place[1]) % window, (window - place[2]) % window)
        probe_total[0] += term[0]
        probe_total[1] += term[1]


def whole(shape):
    return pl.BlockSpec(shape, lambda slot: (0,) * len(shape))


def call(body, capacity, window, layer, operands, specs, outs, out_specs, name, weight=1):
    block = (2, window, window)
    passes = weight * 2 * 12 * 2 * window**3
    return pl.pallas_call(
        body,
        grid=(capacity,),
        in_specs=[
            pl.BlockSpec(memory_space=SMEM),
            pl.BlockSpec(memory_space=SMEM),
            pl.BlockSpec((1, 2, 2 * window, window), lambda slot: (layer, 0, 0, 0)),
            whole(block),
            whole(block),
            whole(block),
            whole(block),
            *specs,
        ],
        out_shape=outs,
        out_specs=out_specs,
        name=name,
        compiler_params=pltpu.CompilerParams(vmem_limit_bytes=LIMIT),
        cost_estimate=pl.CostEstimate(
            flops=capacity * passes, bytes_accessed=8 * 1024 * 1024, transcendentals=0
        ),
    )(*operands)


def from_behind(value, axis, steps):
    count = lax.axis_size(axis)
    leading, last = (max(0, -steps), min(count, count - steps))
    return lax.ppermute(value, axis, [(source, source + steps) for source in range(leading, last)])


def around(value, steps):
    count = lax.axis_size("col")
    return lax.ppermute(value, "col", [(i, i // 4 * 4 + (i + steps) % 4) for i in range(count)])


def across(value, moved, steps):
    edge = 3 if steps < 0 else 0
    count = lax.axis_size("col")
    pairs = [(i, i + 4 * steps) for i in range(edge, count, 4) if 0 <= i + 4 * steps < count]
    passed = lax.ppermute(value, "col", pairs)
    return jnp.where(lax.axis_index("col") % 4 == edge, passed, moved)


def after(value, *earlier):
    for other in earlier:
        other = other.reshape(-1, other.shape[-1])
        value = value + 0.0 * other[: value.shape[0]]
    return value


def exchange(value, axis, bit):
    return lax.ppermute(value, axis, [(i, i ^ bit) for i in range(lax.axis_size(axis))])


def bits(axis, low):
    place = lax.axis_index(axis)
    return place & low != 0, place & (2 * low) != 0


def ordered(pieces, swaps):
    for step, swap in zip((1, 2), swaps):
        pieces = [jnp.where(swap, pieces[k ^ step], pieces[k]) for k in range(len(pieces))]
    return pieces


def sum_chip(value, *earlier):
    value = after(value.reshape(-1, value.shape[-1]), *earlier)
    core = lax.axis_index("row") & 1 != 0
    low, high = jnp.split(value, 2)
    return jnp.where(core, high, low) + exchange(jnp.where(core, low, high), "row", 1)


def sum_everywhere(value, shape, waits):
    core = lax.axis_index("row") & 1 != 0
    value = after(value, *waits[1])
    swaps = bits("col", 8)
    parts = ordered(jnp.split(value, 4), swaps)
    others = [exchange(parts[k], "col", 8 * k) for k in (1, 2, 3)]
    value = (parts[0] + others[0]) + (others[1] + others[2])
    for at, (axis, low) in enumerate((("col", 1), ("row", 2))):
        value = after(value, *waits[at + 2])
        others = [exchange(value, axis, k * low) for k in (1, 2, 3)]
        value = (value + others[0]) + (others[1] + others[2])
    value = after(value, *waits[4])
    value = value + exchange(value, "col", 4)
    value = after(value, *waits[5])
    others = [exchange(value, "col", 8 * k) for k in (1, 2, 3)]
    value = jnp.concatenate(ordered([value, *others], swaps))
    other = exchange(value, "row", 1)
    value = jnp.concatenate([jnp.where(core, other, value), jnp.where(core, value, other)])
    return value.reshape(shape)


def per_device(object_field, probe, prop_phase, slot_count, slot_offset, intensity):
    window = probe.shape[-1]
    capacity = intensity.shape[2]
    offsets = slot_offset[0, 0]
    measured = reorder(intensity[0, 0])
    prop_phase = reorder(prop_phase[None])[0]
    tables = jnp.asarray(dft_blocks(window))
    kernel = jnp.stack([jnp.cos(prop_phase), jnp.sin(prop_phase)])
    block = (2, window, window)
    f32 = jnp.float32
    per_slot = jax.ShapeDtypeStruct((capacity, *block), f32)
    slot_spec = pl.BlockSpec((1, *block), lambda slot: (slot, 0, 0, 0))
    table_spec = whole(tables.shape)
    total_shape = (3, 2, *block)
    total = jax.ShapeDtypeStruct(total_shape, f32)

    rows, columns = lax.axis_size("row"), lax.axis_size("col")

    def between(value, move):
        pairs = []
        for row in range(rows):
            for column in range(columns):
                to_row, to_column = move(row, column)
                if 0 <= to_row < rows and 0 <= to_column < columns:
                    pairs.append((row * columns + column, to_row * columns + to_column))
        return lax.ppermute(value, ("row", "col"), pairs)

    def halo(field):
        top, bottom = field[:, :, :window], field[:, :, window:]
        right_top = from_behind(top, "col", -1)
        below = from_behind(top, "row", -1)
        moved = around(bottom, -1)
        near_corner = between(right_top, lambda r, c: (r - 1 if r % 2 else -1, c))
        far_corner = between(below, lambda r, c: (r if r % 2 else -1, c - 1))
        right_bottom = across(moved, moved, -1)
        return right_top, right_bottom, below, near_corner + far_corner

    def send_down(total):
        return from_behind(total[2], "row", 1), around(total[1, 1], 1)

    near = tuple(part[0] for part in halo(object_field[:1]))
    far = tuple(part[0] for part in halo(object_field[1:]))
    first = (slot_count, offsets, object_field)
    arriving = call(
        arrive_kernel, capacity, window, 0,
        (*first, *near, probe, kernel, tables),
        (whole(block), whole(block), table_spec),
        per_slot, slot_spec, "arrive",
    )
    last_total, leaving = call(
        misfit_kernel, capacity, window, 1,
        (*first, *far, arriving, measured, tables),
        (slot_spec, pl.BlockSpec((1, window, window), lambda slot: (slot, 0, 0)), table_spec),
        (total, per_slot), (whole(total_shape), slot_spec), "misfit",
    )
    first_total, probe_total = call(
        leave_kernel, capacity, window, 0,
        (*first, *near, probe, kernel, leaving, tables),
        (whole(block), whole(block), slot_spec, table_spec),
        (total, jax.ShapeDtypeStruct(block, f32)), (whole(total_shape), whole(block)), "leave", 8,
    )
    def finish(total, below, moved):
        left_top = from_behind(total[0, 1] + below[1], "col", 1)
        left_bottom = across(moved, moved, 1)
        grad = [total[0, 0] + below[0] + left_top, total[1, 0] + left_bottom]
        return jnp.concatenate(grad, axis=1), (left_top, left_bottom)

    last_down = send_down(last_total)
    first_down = send_down(first_total)
    chip_sum = sum_chip(probe_total, last_down[1])
    last_grad, last_over = finish(last_total, *(part + 0.0 * chip_sum for part in last_down))
    first_grad, first_over = finish(first_total, *first_down)
    waits = ((), (last_down[0],), (first_down[1],), (first_down[0],), last_over, ())
    probe_grad = sum_everywhere(chip_sum, block, waits)
    return (jnp.stack([first_grad, last_grad]), probe_grad)


def solution(mesh):
    return jax.shard_map(
        per_device,
        mesh=mesh,
        in_specs=(
            P(None, None, "row", "col"),
            P(),
            P(),
            P("row", "col"),
            P("row", "col", None, None),
            P("row", "col", None, None, None),
        ),
        out_specs=(P(None, None, "row", "col"), P()),
        check_vma=False,
    )
```
